32 devices in a mesh: req: 8 (over z, x), mlp: 4 (over y, core).
Axes of the slice: x: 2, y: 2, z: 4, core: 2. Of those that a mesh axis runs over, the one named last changes fastest.
Arguments:
- hidden_in: bfloat16 [1024, 4096], P('req'), may hold values from -6 to 6
- attn_gain: bfloat16 [4096], replicated, may hold values from 0.5 to 1.5
- w_query: bfloat16 [4096, 2048], P(None, 'mlp'), may hold values from -0.09375 to 0.09375
- w_key: bfloat16 [4096, 512], P(None, 'mlp'), may hold values from -0.09375 to 0.09375
- w_value: bfloat16 [4096, 512], P(None, 'mlp'), may hold values from -0.09375 to 0.09375
- w_out: bfloat16 [2048, 4096], P('mlp'), may hold values from -0.125 to 0.125
- mlp_gain: bfloat16 [4096], replicated, may hold values from 0.5 to 1.5
- w_gate: bfloat16 [4096, 14336], P('mlp', 'req'), may hold values from -0.09375 to 0.09375
- w_up: bfloat16 [4096, 14336], P('mlp', 'req'), may hold values from -0.09375 to 0.09375
- w_down: bfloat16 [14336, 4096], P('req', 'mlp'), may hold values from -0.046875 to 0.046875
- prefix_kv: bfloat16 [16384, 2, 512], P('req', None, 'mlp'), may hold values from -512 to 512
- suffix_lengths: int32 [8, 4], P('req'), may hold values from 1 to 125, as said below
- prefix_owner: int32 [2, 4], replicated, may hold values from 0 to 3, each once within a row
Outputs:
- hidden_out: bfloat16 [1024, 4096], P('req', 'mlp')
- suffix_kv: bfloat16 [1024, 2, 512], P('req', None, 'mlp')
The draws below stay inside these ranges and needn't reach their ends.
Inputs may be any that keep to these rules, and one draw needn't show every extreme that they name: `suffix_lengths`: the lengths of one index of req sum to at most 128; in every draw some index sums to exactly 128. `prefix_owner`: each row is a permutation.
All inputs are finite; a program needn't handle non-finite values.
Results may differ from the reference program's by a relative error of at most 0.02.
The reference program's roundings to bfloat16 on the way count: a program that leaves them out, or rounds other values in their place, can miss the bound.
Values may be sent and summed in bfloat16 or wider, within the bound.
A program may use at most 128 MiB of HBM per device.

```python
import math
import jax
import jax.numpy as jnp
from jax import lax

D = 4096
FF = 14336
HEAD_DIM = 128
HEADS_W = 16
KV_W = 4
PREFIX = 8192
GSPAN = 4
CAP = 128
REQ_DEV = 4
GROUPS = 2
PB = 2048
ROWS = 1024
N_REQ = 8


def draw_suffix_lengths(key, part):
    short_most = CAP // (2 * REQ_DEV)
    key_len, key_pick, key_slot = jax.random.split(key, 3)
    shorts = jax.random.randint(key_len, (N_REQ, REQ_DEV), 1, short_most + 1)
    order = jax.random.permutation(key_pick, N_REQ)
    heavy = max(1, N_REQ // 8)
    is_long = jnp.zeros((N_REQ,), jnp.int32).at[order[:heavy]].set(1)
    is_first = jnp.arange(N_REQ) == order[0]
    shorts = jnp.where(is_first[:, None], 1, shorts)
    where_long = jax.random.randint(key_slot, (N_REQ,), 0, REQ_DEV)
    at_slot = (jnp.arange(REQ_DEV)[None, :] == where_long[:, None]).astype(jnp.int32)
    others = jnp.sum(shorts * (1 - at_slot), axis=1)
    long_len = CAP - others
    result = jnp.where(is_long[:, None] * at_slot > 0, long_len[:, None], shorts)
    return result.astype(jnp.int32)


def draw_prefix_kv(key, part):
    key_k, key_v = jax.random.split(key, 2)
    block_rows = PREFIX // GSPAN
    rows_all = N_REQ * block_rows
    width = KV_W * HEAD_DIM
    shape = (rows_all, width)
    keys_raw = jnp.clip(2.5 * jax.random.normal(key_k, shape, jnp.float32), -15.0, 15.0)
    values_raw = jnp.clip(jax.random.normal(key_v, shape, jnp.float32), -6.0, 6.0)
    return jnp.stack([keys_raw, values_raw], axis=1).astype(jnp.bfloat16)


def block_levels(stream_key, dims, cuts, smallest, top_value):
    def one(axis_at, shards_of):
        heights = jax.random.uniform(jax.random.fold_in(jax.random.fold_in(stream_key, 6), axis_at), (shards_of,), jnp.float32, smallest / len(cuts), top_value / len(cuts))
        return jnp.repeat(jnp.exp(heights), dims[axis_at] // shards_of).reshape((-1,) + (1,) * (len(dims) - axis_at - 1))

    level = one(*cuts[0])
    for cut in cuts[1:]:
        level = level * one(*cut)
    return level


def bell_draw(rng, extent, spread, limit, shards=(), kind=jnp.bfloat16):
    array = jax.random.normal(rng, extent, jnp.float32) * spread
    if len(shards) > 0:
        array = block_levels(rng, extent, shards, -0.22, 0.18) * array
    return jnp.clip(array, min=-limit, max=limit).astype(kind)


def setup_inputs(seed: int = 0) -> dict:
    keys = jax.random.split(jax.random.key(seed), 14)
    hidden_in = bell_draw(keys[0], (ROWS, D), 1.0, 6.0, ((0, 8),))
    attn_gain = jnp.clip(1.0 + 0.1 * jax.random.normal(keys[1], (D,), jnp.float32), 0.5, 1.5).astype(jnp.bfloat16)
    w_query = bell_draw(keys[2], (D, HEADS_W * HEAD_DIM), D ** -0.5, 0.09375, ((1, 4),))
    w_key = bell_draw(keys[3], (D, KV_W * HEAD_DIM), D ** -0.5, 0.09375, ((1, 4),))
    w_value = bell_draw(keys[4], (D, KV_W * HEAD_DIM), D ** -0.5, 0.09375, ((1, 4),))
    w_out = bell_draw(keys[5], (HEADS_W * HEAD_DIM, D), (HEADS_W * HEAD_DIM) ** -0.5, 0.125, ((0, 4),))
    mlp_gain = jnp.clip(1.0 + 0.1 * jax.random.normal(keys[6], (D,), jnp.float32), 0.5, 1.5).astype(jnp.bfloat16)
    w_gate = bell_draw(keys[7], (D, FF), D ** -0.5, 0.09375, ((0, 4), (1, 8)))
    w_up = bell_draw(keys[8], (D, FF), D ** -0.5, 0.09375, ((0, 4), (1, 8)))
    w_down = bell_draw(keys[9], (FF, D), FF ** -0.5, 0.046875, ((0, 8), (1, 4)))
    prefix_kv = draw_prefix_kv(jax.random.fold_in(keys[13], 71), 0)
    suffix_lengths = draw_suffix_lengths(jax.random.fold_in(keys[13], 71), 0)
    prefix_owner = jax.vmap(lambda own: jax.random.permutation(own, GSPAN))(jax.random.split(keys[12], GROUPS)).reshape((GROUPS, GSPAN)).astype(jnp.int32)
    return dict(hidden_in=hidden_in, attn_gain=attn_gain, w_query=w_query, w_key=w_key, w_value=w_value, w_out=w_out, mlp_gain=mlp_gain, w_gate=w_gate, w_up=w_up, w_down=w_down, prefix_kv=prefix_kv, suffix_lengths=suffix_lengths, prefix_owner=prefix_owner)


rope_base = 500000.0
eps = 1e-05

def rope(values, positions):
    half = values.shape[-1] // 2
    freq = rope_base ** (-jnp.arange(half, dtype=jnp.float32) * 2.0 / values.shape[-1])
    angle = positions.astype(jnp.float32)[:, None] * freq[None, :]
    cosine = jnp.cos(angle)[:, None, :]
    sine = jnp.sin(angle)[:, None, :]
    former = values[..., :half]
    latter = values[..., half:]
    return jnp.concatenate([former * cosine - latter * sine, latter * cosine + former * sine], axis=-1)

def rms_norm(values, gain):
    return values * lax.rsqrt(lax.optimization_barrier(jnp.mean(values * values, axis=-1, keepdims=True)) + eps) * gain.astype(jnp.float32)

def slot_layout(lengths, slot_count):
    ends = jnp.cumsum(lengths)
    starts = ends - lengths
    slot_ids = jnp.arange(slot_count, dtype=jnp.int32)
    request_of = lax.optimization_barrier(jnp.sum((slot_ids[:, None] >= ends[None, :]).astype(jnp.int32), axis=1))
    picks = (request_of[:, None] == jnp.arange(lengths.shape[0], dtype=jnp.int32)[None, :]).astype(jnp.int32)
    start_of = lax.optimization_barrier(jnp.sum(picks * starts[None, :], axis=1))
    positions = PREFIX + slot_ids - start_of
    return (request_of, request_of < lengths.shape[0], positions)

def reference(hidden_in, attn_gain, w_query, w_key, w_value, w_out, mlp_gain, w_gate, w_up, w_down, prefix_kv, suffix_lengths, prefix_owner):
    group = HEADS_W // KV_W
    request_all, live_all, position_all = jax.vmap(lambda lengths: slot_layout(lengths, CAP))(suffix_lengths)
    live_flat = live_all.reshape(ROWS)
    position_flat = position_all.reshape(ROWS)
    hidden_f = hidden_in.astype(jnp.float32)
    normed = rms_norm(hidden_f, attn_gain).astype(jnp.bfloat16)
    query_rows = rope(jnp.dot(normed, w_query, preferred_element_type=jnp.float32).reshape(ROWS, HEADS_W, HEAD_DIM), position_flat).astype(jnp.bfloat16)
    key_rows = rope(jnp.dot(normed, w_key, preferred_element_type=jnp.float32).reshape(ROWS, KV_W, HEAD_DIM), position_flat).astype(jnp.bfloat16)
    value_rows = jnp.dot(normed, w_value, preferred_element_type=jnp.float32).astype(jnp.bfloat16).reshape(ROWS, KV_W, HEAD_DIM)
    stacked_kv = jnp.stack([key_rows.reshape(ROWS, KV_W * HEAD_DIM), value_rows.reshape(ROWS, KV_W * HEAD_DIM)], axis=1)
    suffix_kv = jnp.where(live_flat[:, None, None], stacked_kv, jnp.zeros_like(stacked_kv))
    stored = prefix_kv.reshape(GROUPS, GSPAN, PB, 2, KV_W * HEAD_DIM)
    ordered = jax.vmap(lambda blocks, owners: blocks[owners])(stored, prefix_owner)
    prefix_raw = ordered[:, :, :, 0].reshape(GROUPS, PREFIX, KV_W, HEAD_DIM).astype(jnp.float32)
    prefix_pos = jnp.arange(PREFIX, dtype=jnp.int32)
    prefix_keys = jax.vmap(lambda raw: rope(raw, prefix_pos))(prefix_raw).astype(jnp.bfloat16)
    prefix_values = ordered[:, :, :, 1].reshape(GROUPS, PREFIX, KV_W, HEAD_DIM)

    def attend(index):
        queries_here = lax.dynamic_slice_in_dim(query_rows, index * CAP, CAP, 0)
        keys_here = lax.dynamic_slice_in_dim(key_rows, index * CAP, CAP, 0)
        values_here = lax.dynamic_slice_in_dim(value_rows, index * CAP, CAP, 0)
        group_id = index // GSPAN
        keys_all = jnp.concatenate([lax.dynamic_index_in_dim(prefix_keys, group_id, 0, keepdims=False), keys_here], axis=0)
        values_all = jnp.concatenate([lax.dynamic_index_in_dim(prefix_values, group_id, 0, keepdims=False), values_here], axis=0)
        keys_rep = jnp.repeat(keys_all, group, axis=1)
        values_rep = jnp.repeat(values_all, group, axis=1)
        scores = jnp.einsum('qhd,khd->hqk', queries_here.astype(jnp.float32), keys_rep.astype(jnp.float32)) / math.sqrt(HEAD_DIM)
        request_here = lax.dynamic_index_in_dim(request_all, index, 0, keepdims=False)
        slot_ids = jnp.arange(CAP, dtype=jnp.int32)
        allowed = (request_here[:, None] == request_here[None, :]) & (slot_ids[None, :] <= slot_ids[:, None])
        mask = jnp.concatenate([jnp.ones((CAP, PREFIX), dtype=bool), allowed], axis=1)
        scores = jnp.where(mask[None], scores, -jnp.inf)
        peak = lax.optimization_barrier(jnp.max(scores, axis=-1, keepdims=True))
        weights = jnp.exp(scores - peak)
        weight_sum = lax.optimization_barrier(jnp.sum(weights, axis=-1))
        probs = weights.astype(jnp.bfloat16)
        mixed = jnp.einsum('hqk,khd->qhd', probs.astype(jnp.float32), values_rep.astype(jnp.float32))
        result = mixed / jnp.transpose(weight_sum)[:, :, None]
        return result.astype(jnp.bfloat16).reshape(CAP, HEADS_W * HEAD_DIM)
    attended = lax.map(attend, jnp.arange(N_REQ, dtype=jnp.int32)).reshape(ROWS, HEADS_W * HEAD_DIM)
    residual = (hidden_f + jnp.dot(attended, w_out, preferred_element_type=jnp.float32)).astype(jnp.bfloat16)
    normed_mlp = rms_norm(residual.astype(jnp.float32), mlp_gain).astype(jnp.bfloat16)
    gate = jnp.dot(normed_mlp, w_gate, preferred_element_type=jnp.float32)
    up_part = jnp.dot(normed_mlp, w_up, preferred_element_type=jnp.float32)
    act = (jax.nn.silu(gate) * up_part).astype(jnp.bfloat16)
    act_blocks = jnp.transpose(act.reshape(ROWS, N_REQ, FF // N_REQ), (1, 0, 2))
    down_blocks = w_down.reshape(N_REQ, FF // N_REQ, D)

    def add_block(carry, pair):
        term = jnp.dot(pair[0], pair[1], preferred_element_type=jnp.float32).astype(jnp.bfloat16)
        term = lax.optimization_barrier(term)
        return (carry + term.astype(jnp.float32), None)
    down, _ = lax.scan(add_block, jnp.zeros((ROWS, D), jnp.float32), (act_blocks, down_blocks))
    total = residual.astype(jnp.float32) + down
    hidden_out = jnp.where(live_flat[:, None], total, 0.0).astype(jnp.bfloat16)
    return (hidden_out, suffix_kv)
```

```python
import math

import jax
import jax.numpy as jnp
from jax import lax
from jax.sharding import PartitionSpec as P

HEAD_DIM = 128
PREFIX = 8192
GSPAN = 4


rope_base = 500000.0
eps = 1e-05


def from_xor(value, axis, mask):
    pairs = [(source, source ^ mask) for source in range(lax.axis_size(axis))]
    return lax.ppermute(value, axis, pairs)


def to_column(value, shift):
    size = lax.axis_size("req")
    pairs = [(source, (source + 2 * shift) % size) for source in range(size)]
    return lax.ppermute(value, "req", pairs)


def rope(values, positions):
    half = values.shape[-1] // 2
    freq = rope_base ** (-jnp.arange(half, dtype=jnp.float32) * 2.0 / values.shape[-1])
    angle = positions.astype(jnp.float32)[:, None] * freq[None, :]
    cosine = jnp.cos(angle)[:, None, :]
    sine = jnp.sin(angle)[:, None, :]
    former = values[..., :half]
    latter = values[..., half:]
    return jnp.concatenate(
        [former * cosine - latter * sine, latter * cosine + former * sine], axis=-1
    )


def rms_norm(values, gain):
    return (
        values
        * lax.rsqrt(jnp.mean(values * values, axis=-1, keepdims=True) + eps)
        * gain.astype(jnp.float32)
    )


def slot_layout(lengths, slot_count):
    ends = jnp.cumsum(lengths)
    starts = ends - lengths
    slot_ids = jnp.arange(slot_count, dtype=jnp.int32)
    request_of = jnp.sum((slot_ids[:, None] >= ends[None, :]).astype(jnp.int32), axis=1)
    picks = (request_of[:, None] == jnp.arange(lengths.shape[0], dtype=jnp.int32)[None, :]).astype(
        jnp.int32
    )
    start_of = jnp.sum(picks * starts[None, :], axis=1)
    positions = PREFIX + slot_ids - start_of
    return (request_of, request_of < lengths.shape[0], positions)


def partial_attention(grouped_queries, key_block, value_block, allowed):
    scores = jnp.einsum(
        "qkgd,nkd->kgqn", grouped_queries, key_block, preferred_element_type=jnp.float32
    ) / math.sqrt(grouped_queries.shape[-1])
    if allowed is not None:
        scores = jnp.where(allowed[None, None], scores, -jnp.inf)
    peak = jnp.max(scores, axis=-1)
    weights = jnp.exp(scores - peak[..., None])
    weight_sum = jnp.sum(weights, axis=-1)
    summed = jnp.einsum(
        "kgqn,nkd->kgqd",
        weights.astype(jnp.bfloat16),
        value_block,
        preferred_element_type=jnp.float32,
    )
    return (summed / weight_sum[..., None], peak + jnp.log(weight_sum))


def halves(value, which):
    rows = value.shape[0] // 2
    return (
        lax.dynamic_slice_in_dim(value, which * rows, rows, 0),
        lax.dynamic_slice_in_dim(value, (1 - which) * rows, rows, 0),
    )


def join(mine, other, which):
    return jnp.where(
        which == 0,
        jnp.concatenate([mine, other], axis=0),
        jnp.concatenate([other, mine], axis=0),
    )


def shards(
    hidden_in,
    attn_gain,
    w_query,
    w_key,
    w_value,
    w_out,
    mlp_gain,
    w_gate,
    w_up,
    w_down,
    prefix_kv,
    suffix_lengths,
    prefix_owner,
):
    f32 = jnp.float32
    bf16 = jnp.bfloat16
    slots_here = hidden_in.shape[0]
    width = hidden_in.shape[1]
    head_dim = HEAD_DIM
    kv_heads = w_key.shape[1] // head_dim
    q_heads = w_query.shape[1] // head_dim
    group = q_heads // kv_heads
    block_len = prefix_kv.shape[0]
    width_part = w_gate.shape[0]
    unit_count = w_gate.shape[1]
    columns = lax.axis_size("req") // 2
    mlp_at = lax.axis_index("mlp")
    low, high = mlp_at % 2, mlp_at // 2
    width_start = mlp_at * width_part
    request_of, live, positions = slot_layout(suffix_lengths[0], slots_here)
    hidden_f = hidden_in.astype(f32)
    normed = rms_norm(hidden_f, attn_gain).astype(bf16)
    query_rows = rope(
        jnp.dot(normed, w_query, preferred_element_type=f32).reshape(
            slots_here, q_heads, head_dim
        ),
        positions,
    ).astype(bf16)
    all_queries = [query_rows] + [from_xor(query_rows, "req", mask) for mask in range(1, GSPAN)]
    key_rows = rope(
        jnp.dot(normed, w_key, preferred_element_type=f32).reshape(slots_here, kv_heads, head_dim),
        positions,
    ).astype(bf16)
    value_rows = (
        jnp.dot(normed, w_value, preferred_element_type=f32)
        .astype(bf16)
        .reshape(slots_here, kv_heads, head_dim)
    )
    place = lax.axis_index("req") % GSPAN
    group_id = lax.axis_index("req") // GSPAN
    owners = lax.dynamic_index_in_dim(prefix_owner, group_id, 0, keepdims=False)
    quarter = jnp.sum(jnp.where(owners == place, jnp.arange(GSPAN, dtype=jnp.int32), 0))
    prefix_pos = quarter * block_len + jnp.arange(block_len, dtype=jnp.int32)
    stored_keys = rope(
        prefix_kv[:, 0].reshape(block_len, kv_heads, head_dim).astype(f32), prefix_pos
    ).astype(bf16)
    stored_values = prefix_kv[:, 1].reshape(block_len, kv_heads, head_dim)
    slot_ids = jnp.arange(slots_here, dtype=jnp.int32)
    allowed = (request_of[:, None] == request_of[None, :]) & (
        slot_ids[None, :] <= slot_ids[:, None]
    )
    outs, tops = [], []
    for mask in range(GSPAN):
        grouped = all_queries[mask].reshape(slots_here, kv_heads, group, head_dim)
        out, top = partial_attention(grouped, stored_keys, stored_values, None)
        if mask:
            out = from_xor(out.astype(bf16), "req", mask).astype(f32)
            top = from_xor(top, "req", mask)
        outs.append(out)
        tops.append(top)
    out, top = partial_attention(
        query_rows.reshape(slots_here, kv_heads, group, head_dim), key_rows, value_rows, allowed
    )
    outs.append(out)
    tops.append(top)
    highest = tops[0]
    for top in tops[1:]:
        highest = jnp.maximum(highest, top)
    merged, total = 0.0, 0.0
    for out, top in zip(outs, tops):
        share = jnp.exp(top - highest)
        merged += out * share[..., None]
        total += share
    attended = (
        jnp.transpose(merged / total[..., None], (2, 0, 1, 3))
        .reshape(slots_here, q_heads * head_dim)
        .astype(bf16)
    )

    def term_part(index):
        start = index * width_part
        return jnp.dot(
            attended,
            lax.dynamic_slice_in_dim(w_out, start, width_part, 1),
            preferred_element_type=f32,
        )

    away, home = (1 - high) * 2, high * 2
    away_in = from_xor(term_part(away + 1 - low).astype(bf16), "mlp", 1)
    home_in = from_xor(term_part(home + 1 - low).astype(bf16), "mlp", 1)
    away_out = (term_part(away + low) + away_in.astype(f32)).astype(bf16)
    across = from_xor(away_out, "mlp", 2)
    head_total = term_part(home + low) + home_in.astype(f32) + across.astype(f32)
    hidden_part = lax.dynamic_slice_in_dim(hidden_in, width_start, width_part, 1)
    residual_part = (hidden_part.astype(f32) + head_total).astype(bf16)
    residual_f = residual_part.astype(f32)
    squares = jnp.sum(residual_f * residual_f, axis=-1)
    squares += from_xor(squares, "mlp", 1)
    squares += from_xor(squares, "mlp", 2)
    gain_part = lax.dynamic_slice_in_dim(mlp_gain, width_start, width_part, 0)
    normed_part = (
        residual_f * lax.rsqrt(squares / width + eps)[:, None] * gain_part.astype(f32)
    ).astype(bf16)

    pair_at = lax.axis_index("req") % 2
    arrived = [normed_part] + [to_column(normed_part, -shift) for shift in range(1, columns)]
    down = 0.0
    for shift in range(columns):
        mine = arrived[shift]
        rows = join(mine, from_xor(mine, "req", 1), pair_at)
        kept_rows, sent_rows = halves(rows, low)
        sent = jnp.concatenate(
            [
                jnp.dot(sent_rows, w_gate, preferred_element_type=f32).astype(bf16),
                jnp.dot(sent_rows, w_up, preferred_element_type=f32).astype(bf16),
            ],
            axis=1,
        )
        sums = from_xor(sent, "mlp", 1).astype(f32) + jnp.concatenate(
            [
                jnp.dot(kept_rows, w_gate, preferred_element_type=f32),
                jnp.dot(kept_rows, w_up, preferred_element_type=f32),
            ],
            axis=1,
        )
        kept_sums, sent_sums = halves(sums, high)
        gate_up = kept_sums + from_xor(sent_sums.astype(bf16), "mlp", 2).astype(f32)
        act = (jax.nn.silu(gate_up[:, :unit_count]) * gate_up[:, unit_count:]).astype(bf16)
        act = join(act, from_xor(act, "mlp", 2), high)
        act = join(act, from_xor(act, "mlp", 1), low)
        kept_act, sent_act = halves(act, pair_at)
        term_in = from_xor(
            jnp.dot(sent_act, w_down, preferred_element_type=f32).astype(bf16), "req", 1
        )
        term = jnp.dot(kept_act, w_down, preferred_element_type=f32) + term_in.astype(f32)
        if shift:
            term = to_column(term.astype(bf16), shift).astype(f32)
        down += term
    hidden_out = jnp.where(live[:, None], residual_f + down, 0.0).astype(bf16)
    stacked_kv = jnp.stack(
        [
            key_rows.reshape(slots_here, kv_heads * head_dim),
            value_rows.reshape(slots_here, kv_heads * head_dim),
        ],
        axis=1,
    )
    suffix_kv = jnp.where(live[:, None, None], stacked_kv, jnp.zeros_like(stacked_kv))
    return (hidden_out, suffix_kv)


def solution(mesh):
    placed = (
        P("req", None),
        P(),
        P(None, "mlp"),
        P(None, "mlp"),
        P(None, "mlp"),
        P("mlp", None),
        P(),
        P("mlp", "req"),
        P("mlp", "req"),
        P("req", "mlp"),
        P("req", None, "mlp"),
        P("req", None),
        P(),
    )
    return jax.shard_map(
        shards,
        mesh=mesh,
        in_specs=placed,
        out_specs=(P("req", "mlp"), P("req", None, "mlp")),
        check_vma=False,
    )
```

```python
import functools
import math

import jax
import jax.numpy as jnp
from jax import lax
from jax.experimental import pallas as pl
from jax.experimental.pallas import tpu as pltpu
from jax.sharding import PartitionSpec as P

HEAD_DIM = 128
PREFIX = 8192
GSPAN = 4


rope_base = 500000.0
eps = 1e-05


def from_xor(value, axis, mask):
    pairs = [(source, source ^ mask) for source in range(lax.axis_size(axis))]
    return lax.ppermute(value, axis, pairs)


def rope(values, positions):
    half = values.shape[-1] // 2
    freq = rope_base ** (-jnp.arange(half, dtype=jnp.float32) * 2.0 / values.shape[-1])
    angle = positions.astype(jnp.float32)[:, None] * freq[None, :]
    cosine = jnp.cos(angle)[:, None, :]
    sine = jnp.sin(angle)[:, None, :]
    former = values[..., :half]
    latter = values[..., half:]
    return jnp.concatenate(
        [former * cosine - latter * sine, latter * cosine + former * sine], axis=-1
    )


def rms_norm(values, gain):
    return (
        values
        * lax.rsqrt(jnp.mean(values * values, axis=-1, keepdims=True) + eps)
        * gain.astype(jnp.float32)
    )


def slot_layout(lengths, slot_count):
    ends = jnp.cumsum(lengths)
    starts = ends - lengths
    slot_ids = jnp.arange(slot_count, dtype=jnp.int32)
    request_of = jnp.sum((slot_ids[:, None] >= ends[None, :]).astype(jnp.int32), axis=1)
    picks = (request_of[:, None] == jnp.arange(lengths.shape[0], dtype=jnp.int32)[None, :]).astype(
        jnp.int32
    )
    start_of = jnp.sum(picks * starts[None, :], axis=1)
    positions = PREFIX + slot_ids - start_of
    return (request_of, request_of < lengths.shape[0], positions)


def partial_attention(grouped_queries, key_block, value_block, allowed):
    scores = jnp.einsum(
        "qkgd,nkd->kgqn", grouped_queries, key_block, preferred_element_type=jnp.float32
    ) / math.sqrt(grouped_queries.shape[-1])
    if allowed is not None:
        scores = jnp.where(allowed[None, None], scores, -jnp.inf)
    peak = jnp.max(scores, axis=-1)
    weights = jnp.exp(scores - peak[..., None])
    weight_sum = jnp.sum(weights, axis=-1)
    summed = jnp.einsum(
        "kgqn,nkd->kgqd",
        weights.astype(jnp.bfloat16),
        value_block,
        preferred_element_type=jnp.float32,
    )
    return (summed / weight_sum[..., None], peak + jnp.log(weight_sum))


def tile_of(size):
    return 256 if size % 256 == 0 else size


def over_tiles(size, body):
    tile = tile_of(size)
    if size == tile:
        body(pl.ds(0, tile))
        return

    @pl.loop(0, size // tile)
    def _(index):
        body(pl.ds(pl.multiple_of(index * tile, tile), tile))


def feed_forward_kernel(
    columns,
    normed_ref,
    residual_ref,
    live_ref,
    gate_hbm,
    up_hbm,
    down_hbm,
    out_ref,
    w_gate,
    w_up,
    w_down,
    rows,
    kept_sums,
    pair_out,
    pair_in,
    across_out,
    across_in,
    act,
    kept_down,
    term_out,
    term_in,
    sum_out,
    sum_in,
    total,
    weight_sems,
    send_sems,
    recv_sems,
):
    f32, bf16 = jnp.float32, jnp.bfloat16
    req, mlp = lax.axis_index("req"), lax.axis_index("mlp")
    column, pair = lax.div(req, 2), lax.rem(req, 2)
    high, low = lax.div(mlp, 2), lax.rem(mlp, 2)
    count = normed_ref.shape[0]
    part = count // 2
    width = normed_ref.shape[1]
    units = w_gate.shape[1]
    pair_peer = (column * 2 + 1 - pair, mlp)
    core_peer = (req, high * 2 + 1 - low)
    across_peer = (req, (1 - high) * 2 + low)

    def column_peer(shift):
        return (lax.rem(column + shift, columns) * 2 + pair, mlp)

    def copy(kind, k, src, dst, peer):
        return pltpu.make_async_remote_copy(
            src_ref=src,
            dst_ref=dst,
            send_sem=send_sems.at[kind, k],
            recv_sem=recv_sems.at[kind, k],
            device_id=peer,
            device_id_type=pl.DeviceIdType.MESH,
        )

    started = []

    def send(kind, k, src, dst, peer):
        descriptor = copy(kind, k, src, dst, peer)
        descriptor.start()
        started.append(descriptor)

    def receive(kind, k, dst, peer):
        copy(kind, k, dst, dst, peer).wait_recv()

    loads = [
        pltpu.make_async_copy(source, target, weight_sems.at[index])
        for index, (source, target) in enumerate(
            [(gate_hbm, w_gate), (up_hbm, w_up), (down_hbm, w_down)]
        )
    ]
    for load in loads:
        load.start()

    barrier = pltpu.get_barrier_semaphore()
    peers = [pair_peer, core_peer, across_peer] + [column_peer(k) for k in range(1, columns)]
    for peer in peers:
        pl.semaphore_signal(barrier, inc=1, device_id=peer, device_id_type=pl.DeviceIdType.MESH)
    pl.semaphore_wait(barrier, len(peers))

    send(1, 0, normed_ref, rows.at[0, pair], pair_peer)
    for k in range(1, columns):
        send(0, k, normed_ref, rows.at[k, pair], column_peer(columns - k))
    rows[0, pair] = normed_ref[...]

    def forward(k):
        receive(0, k, rows.at[k, pair], column_peer(k))
        send(1, k, rows.at[k, pair], rows.at[k, pair], pair_peer)

    def pick(value, which):
        return jnp.where(which == 0, value[:count], value[count:])

    def first_sums(k):
        receive(1, k, rows.at[k, 1 - pair], pair_peer)
        slot = k % 3
        for half, weight in enumerate((w_gate, w_up)):
            if k == 0:
                loads[half].wait()

            def body(at, half=half, weight=weight):
                sums = jnp.dot(
                    rows[k].reshape(2 * count, width), weight[:, at], preferred_element_type=f32
                )
                pair_out[k, half, :, at] = pick(sums, 1 - low).astype(bf16)
                kept_sums[slot, half, :, at] = pick(sums, low)

            over_tiles(units, body)
        send(2, k, pair_out.at[k], pair_in.at[k], core_peer)

    def second_sums(k):
        receive(2, k, pair_in.at[k], core_peer)
        at = pl.ds(pl.multiple_of((1 - high) * part, part), part)
        for half in range(2):
            across_out[k, half] = (
                kept_sums[k % 3, half, at, :] + pair_in[k, half, at, :].astype(f32)
            ).astype(bf16)
        send(3, k, across_out.at[k], across_in.at[k], across_peer)

    mine = low * count + high * part
    swapped = low * count + (1 - high) * part

    def act_rows(k, start):
        return act.at[k, pl.ds(pl.multiple_of(start, part), part), :]

    def activate(k):
        receive(3, k, across_in.at[k], across_peer)
        at = pl.ds(pl.multiple_of(high * part, part), part)
        gate, up = [
            kept_sums[k % 3, half, at, :]
            + pair_in[k, half, at, :].astype(f32)
            + across_in[k, half].astype(f32)
            for half in range(2)
        ]
        value = (gate / (1.0 + jnp.exp(-gate)) * up).astype(bf16)
        act[k, pl.ds(pl.multiple_of(mine, part), part), :] = value
        send(4, k, act_rows(k, mine), act_rows(k, mine), across_peer)
        send(5, k, act_rows(k, mine), act_rows(k, mine), core_peer)

    def down_terms(k):
        receive(4, k, act_rows(k, swapped), across_peer)
        send(6, k, act_rows(k, swapped), act_rows(k, swapped), core_peer)
        receive(5, k, act_rows(k, (1 - low) * count + high * part), core_peer)
        receive(6, k, act_rows(k, (1 - low) * count + (1 - high) * part), core_peer)
        if k == 0:
            loads[2].wait()

        def body(at):
            terms = jnp.dot(act[k], w_down[:, at], preferred_element_type=f32)
            term_out[k, :, at] = pick(terms, 1 - pair).astype(bf16)
            kept_down[k % 2, :, at] = pick(terms, pair)

        over_tiles(width, body)
        send(7, k, term_out.at[k], term_in.at[k], pair_peer)

    def pass_on(k):
        receive(7, k, term_in.at[k], pair_peer)
        value = kept_down[k % 2] + term_in[k].astype(f32)
        if k == 0:
            total[...] = value
            return
        sum_out[k] = value.astype(bf16)
        send(8, k, sum_out.at[k], sum_in.at[k], column_peer(k))

    for step in range(columns + 4):
        if step < columns:
            first_sums(step)
            second_sums(step)
            if step + 1 < columns:
                forward(step + 1)
        for behind, stage in ((1, activate), (2, down_terms), (3, pass_on)):
            if 0 <= step - behind < columns:
                stage(step - behind)
    down = total[...]
    for k in range(1, columns):
        receive(8, k, sum_in.at[k], column_peer(columns - k))
        down += sum_in[k].astype(f32)
    out_ref[...] = jnp.where(
        live_ref[...] > 0.0, residual_ref[...].astype(f32) + down, 0.0
    ).astype(bf16)
    for descriptor in started:
        descriptor.wait_send()


def feed_forward(normed_part, residual_part, live, w_gate, w_up, w_down):
    bf16, f32 = jnp.bfloat16, jnp.float32
    columns = lax.axis_size("req") // 2
    count, width = normed_part.shape
    units = w_gate.shape[1]
    in_vmem = pl.BlockSpec(memory_space=pltpu.VMEM)
    anywhere = pl.BlockSpec(memory_space=pl.ANY)
    return pl.pallas_call(
        functools.partial(feed_forward_kernel, columns),
        name="feed_forward",
        out_shape=jax.ShapeDtypeStruct((count, width), bf16),
        in_specs=[in_vmem] * 3 + [anywhere] * 3,
        out_specs=in_vmem,
        scratch_shapes=[
            pltpu.VMEM(w_gate.shape, bf16),
            pltpu.VMEM(w_up.shape, bf16),
            pltpu.VMEM(w_down.shape, bf16),
            pltpu.VMEM((columns, 2, count, width), bf16),
            pltpu.VMEM((3, 2, count, units), f32),
            pltpu.VMEM((columns, 2, count, units), bf16),
            pltpu.VMEM((columns, 2, count, units), bf16),
            pltpu.VMEM((columns, 2, count // 2, units), bf16),
            pltpu.VMEM((columns, 2, count // 2, units), bf16),
            pltpu.VMEM((columns, 2 * count, units), bf16),
            pltpu.VMEM((2, count, width), f32),
            pltpu.VMEM((columns, count, width), bf16),
            pltpu.VMEM((columns, count, width), bf16),
            pltpu.VMEM((columns, count, width), bf16),
            pltpu.VMEM((columns, count, width), bf16),
            pltpu.VMEM((count, width), f32),
            pltpu.SemaphoreType.DMA((3,)),
            pltpu.SemaphoreType.DMA((9, columns)),
            pltpu.SemaphoreType.DMA((9, columns)),
        ],
        compiler_params=pltpu.CompilerParams(
            collective_id=0, has_side_effects=True, vmem_limit_bytes=60 * 1024 * 1024
        ),
    )(normed_part, residual_part, live, w_gate, w_up, w_down)


def shards(
    hidden_in,
    attn_gain,
    w_query,
    w_key,
    w_value,
    w_out,
    mlp_gain,
    w_gate,
    w_up,
    w_down,
    prefix_kv,
    suffix_lengths,
    prefix_owner,
):
    f32 = jnp.float32
    bf16 = jnp.bfloat16
    slots_here = hidden_in.shape[0]
    width = hidden_in.shape[1]
    head_dim = HEAD_DIM
    kv_heads = w_key.shape[1] // head_dim
    q_heads = w_query.shape[1] // head_dim
    group = q_heads // kv_heads
    block_len = prefix_kv.shape[0]
    width_part = w_gate.shape[0]
    mlp_at = lax.axis_index("mlp")
    low, high = mlp_at % 2, mlp_at // 2
    width_start = mlp_at * width_part
    request_of, live, positions = slot_layout(suffix_lengths[0], slots_here)
    hidden_f = hidden_in.astype(f32)
    normed = rms_norm(hidden_f, attn_gain).astype(bf16)
    query_rows = rope(
        jnp.dot(normed, w_query, preferred_element_type=f32).reshape(
            slots_here, q_heads, head_dim
        ),
        positions,
    ).astype(bf16)
    all_queries = [query_rows] + [from_xor(query_rows, "req", mask) for mask in range(1, GSPAN)]
    key_rows = rope(
        jnp.dot(normed, w_key, preferred_element_type=f32).reshape(slots_here, kv_heads, head_dim),
        positions,
    ).astype(bf16)
    value_rows = (
        jnp.dot(normed, w_value, preferred_element_type=f32)
        .astype(bf16)
        .reshape(slots_here, kv_heads, head_dim)
    )
    place = lax.axis_index("req") % GSPAN
    group_id = lax.axis_index("req") // GSPAN
    owners = lax.dynamic_index_in_dim(prefix_owner, group_id, 0, keepdims=False)
    quarter = jnp.sum(jnp.where(owners == place, jnp.arange(GSPAN, dtype=jnp.int32), 0))
    prefix_pos = quarter * block_len + jnp.arange(block_len, dtype=jnp.int32)
    stored_keys = rope(
        prefix_kv[:, 0].reshape(block_len, kv_heads, head_dim).astype(f32), prefix_pos
    ).astype(bf16)
    stored_values = prefix_kv[:, 1].reshape(block_len, kv_heads, head_dim)
    slot_ids = jnp.arange(slots_here, dtype=jnp.int32)
    allowed = (request_of[:, None] == request_of[None, :]) & (
        slot_ids[None, :] <= slot_ids[:, None]
    )
    outs, tops = [], []
    for mask in range(GSPAN):
        grouped = all_queries[mask].reshape(slots_here, kv_heads, group, head_dim)
        out, top = partial_attention(grouped, stored_keys, stored_values, None)
        if mask:
            out = from_xor(out.astype(bf16), "req", mask).astype(f32)
            top = from_xor(top, "req", mask)
        outs.append(out)
        tops.append(top)
    out, top = partial_attention(
        query_rows.reshape(slots_here, kv_heads, group, head_dim), key_rows, value_rows, allowed
    )
    outs.append(out)
    tops.append(top)
    highest = tops[0]
    for top in tops[1:]:
        highest = jnp.maximum(highest, top)
    merged, total = 0.0, 0.0
    for out, top in zip(outs, tops):
        share = jnp.exp(top - highest)
        merged += out * share[..., None]
        total += share
    attended = (
        jnp.transpose(merged / total[..., None], (2, 0, 1, 3))
        .reshape(slots_here, q_heads * head_dim)
        .astype(bf16)
    )

    def term_part(index):
        start = index * width_part
        return jnp.dot(
            attended,
            lax.dynamic_slice_in_dim(w_out, start, width_part, 1),
            preferred_element_type=f32,
        )

    away, home = (1 - high) * 2, high * 2
    away_in = from_xor(term_part(away + 1 - low).astype(bf16), "mlp", 1)
    home_in = from_xor(term_part(home + 1 - low).astype(bf16), "mlp", 1)
    away_out = (term_part(away + low) + away_in.astype(f32)).astype(bf16)
    across = from_xor(away_out, "mlp", 2)
    head_total = term_part(home + low) + home_in.astype(f32) + across.astype(f32)
    hidden_part = lax.dynamic_slice_in_dim(hidden_in, width_start, width_part, 1)
    residual_part = (hidden_part.astype(f32) + head_total).astype(bf16)
    residual_f = residual_part.astype(f32)
    squares = jnp.sum(residual_f * residual_f, axis=-1)
    squares += from_xor(squares, "mlp", 1)
    squares += from_xor(squares, "mlp", 2)
    gain_part = lax.dynamic_slice_in_dim(mlp_gain, width_start, width_part, 0)
    normed_part = (
        residual_f * lax.rsqrt(squares / width + eps)[:, None] * gain_part.astype(f32)
    ).astype(bf16)

    hidden_out = feed_forward(
        normed_part, residual_part, live.astype(f32)[:, None], w_gate, w_up, w_down
    )
    stacked_kv = jnp.stack(
        [
            key_rows.reshape(slots_here, kv_heads * head_dim),
            value_rows.reshape(slots_here, kv_heads * head_dim),
        ],
        axis=1,
    )
    suffix_kv = jnp.where(live[:, None, None], stacked_kv, jnp.zeros_like(stacked_kv))
    return (hidden_out, suffix_kv)


def solution(mesh):
    placed = (
        P("req", None),
        P(),
        P(None, "mlp"),
        P(None, "mlp"),
        P(None, "mlp"),
        P("mlp", None),
        P(),
        P("mlp", "req"),
        P("mlp", "req"),
        P("req", "mlp"),
        P("req", None, "mlp"),
        P("req", None),
        P(),
    )
    return jax.shard_map(
        shards,
        mesh=mesh,
        in_specs=placed,
        out_specs=(P("req", "mlp"), P("req", None, "mlp")),
        check_vma=False,
    )
```

```python
import functools
import math

import jax
import jax.numpy as jnp
import numpy as np
from jax import lax
from jax.experimental import pallas as pl
from jax.experimental.pallas import tpu as pltpu
from jax.sharding import PartitionSpec as P

HEAD_DIM = 128
PREFIX = 8192
GSPAN = 4


rope_base = 500000.0
eps = 1e-05


def from_xor(value, axis, mask):
    pairs = [(source, source ^ mask) for source in range(lax.axis_size(axis))]
    return lax.ppermute(value, axis, pairs)


def rope(values, positions):
    half = values.shape[-1] // 2
    freq = rope_base ** (-jnp.arange(half, dtype=jnp.float32) * 2.0 / values.shape[-1])
    angle = positions.astype(jnp.float32)[:, None] * freq[None, :]
    cosine = jnp.cos(angle)[:, None, :]
    sine = jnp.sin(angle)[:, None, :]
    former = values[..., :half]
    latter = values[..., half:]
    return jnp.concatenate(
        [former * cosine - latter * sine, latter * cosine + former * sine], axis=-1
    )


def prefix_tables(head_dim):
    half = head_dim // 2
    exponents = -np.arange(half, dtype=np.float32) * np.float32(2.0) / np.float32(head_dim)
    freq = np.power(np.float32(rope_base), exponents).astype(np.float32)
    angle = np.arange(PREFIX, dtype=np.float32)[:, None] * freq[None, :]
    return np.concatenate([np.cos(angle), np.sin(angle)], axis=1).astype(np.float32)


def rms_norm(values, gain):
    return (
        values
        * lax.rsqrt(jnp.mean(values * values, axis=-1, keepdims=True) + eps)
        * gain.astype(jnp.float32)
    )


def slot_layout(lengths, slot_count):
    ends = jnp.cumsum(lengths)
    starts = ends - lengths
    slot_ids = jnp.arange(slot_count, dtype=jnp.int32)
    request_of = jnp.sum((slot_ids[:, None] >= ends[None, :]).astype(jnp.int32), axis=1)
    picks = (request_of[:, None] == jnp.arange(lengths.shape[0], dtype=jnp.int32)[None, :]).astype(
        jnp.int32
    )
    start_of = jnp.sum(picks * starts[None, :], axis=1)
    positions = PREFIX + slot_ids - start_of
    return (request_of, request_of < lengths.shape[0], positions)


def partial_attention(grouped_queries, key_block, value_block, allowed):
    scores = jnp.einsum(
        "qkgd,nkd->kgqn", grouped_queries, key_block, preferred_element_type=jnp.float32
    ) / math.sqrt(grouped_queries.shape[-1])
    if allowed is not None:
        scores = jnp.where(allowed[None, None], scores, -jnp.inf)
    peak = jnp.max(scores, axis=-1)
    weights = jnp.exp(scores - peak[..., None])
    weight_sum = jnp.sum(weights, axis=-1)
    summed = jnp.einsum(
        "kgqn,nkd->kgqd",
        weights.astype(jnp.bfloat16),
        value_block,
        preferred_element_type=jnp.float32,
    )
    return (summed / weight_sum[..., None], peak + jnp.log(weight_sum))


def tile_of(size):
    return 256 if size % 256 == 0 else size


def over_tiles(size, body):
    tile = tile_of(size)
    if size == tile:
        body(pl.ds(0, tile))
        return

    @pl.loop(0, size // tile)
    def _(index):
        body(pl.ds(pl.multiple_of(index * tile, tile), tile))


def feed_forward_kernel(
    columns,
    normed_ref,
    residual_ref,
    live_ref,
    gate_hbm,
    up_hbm,
    down_hbm,
    out_ref,
    w_gate,
    w_up,
    w_down,
    rows,
    kept_sums,
    pair_out,
    pair_in,
    across_out,
    across_in,
    act,
    kept_down,
    term_out,
    term_in,
    sum_out,
    sum_in,
    total,
    weight_sems,
    send_sems,
    recv_sems,
):
    f32, bf16 = jnp.float32, jnp.bfloat16
    req, mlp = lax.axis_index("req"), lax.axis_index("mlp")
    column, pair = lax.div(req, 2), lax.rem(req, 2)
    high, low = lax.div(mlp, 2), lax.rem(mlp, 2)
    pieces = rows.shape[0] // columns
    chunks = columns * pieces
    count = normed_ref.shape[0] // pieces
    part = count // 2
    width = normed_ref.shape[1]
    units = w_gate.shape[1]
    pair_peer = (column * 2 + 1 - pair, mlp)
    core_peer = (req, high * 2 + 1 - low)
    across_peer = (req, (1 - high) * 2 + low)

    def column_peer(mask):
        other = column
        for bit in range(columns.bit_length() - 1):
            if mask >> bit & 1:
                other += (1 - 2 * lax.rem(lax.div(column, 1 << bit), 2)) * (1 << bit)
        return (other * 2 + pair, mlp)

    def piece(k):
        return pl.ds(k % pieces * count, count)

    def copy(kind, k, src, dst, peer):
        return pltpu.make_async_remote_copy(
            src_ref=src,
            dst_ref=dst,
            send_sem=send_sems.at[kind, k],
            recv_sem=recv_sems.at[kind, k],
            device_id=peer,
            device_id_type=pl.DeviceIdType.MESH,
        )

    started = []

    def send(kind, k, src, dst, peer):
        descriptor = copy(kind, k, src, dst, peer)
        descriptor.start()
        started.append(descriptor)

    def receive(kind, k, dst, peer):
        copy(kind, k, dst, dst, peer).wait_recv()

    loads = [
        pltpu.make_async_copy(source, target, weight_sems.at[index])
        for index, (source, target) in enumerate(
            [(gate_hbm, w_gate), (up_hbm, w_up), (down_hbm, w_down)]
        )
    ]
    for load in loads:
        load.start()

    barrier = pltpu.get_barrier_semaphore()
    peers = [pair_peer, core_peer, across_peer] + [column_peer(k) for k in range(1, columns)]
    for peer in peers:
        pl.semaphore_signal(barrier, inc=1, device_id=peer, device_id_type=pl.DeviceIdType.MESH)
    pl.semaphore_wait(barrier, len(peers))

    for k in range(chunks):
        if k < pieces:
            send(1, k, normed_ref.at[piece(k)], rows.at[k, pair], pair_peer)
            rows[k, pair] = normed_ref[piece(k)]
        else:
            send(0, k, normed_ref.at[piece(k)], rows.at[k, pair], column_peer(k // pieces))

    def forward(k):
        receive(0, k, rows.at[k, pair], column_peer(k // pieces))
        send(1, k, rows.at[k, pair], rows.at[k, pair], pair_peer)

    def pick(value, which):
        return jnp.where(which == 0, value[:count], value[count:])

    def first_sums(k):
        receive(1, k, rows.at[k, 1 - pair], pair_peer)
        slot = k % 4
        for half, weight in enumerate((w_gate, w_up)):
            if k == 0:
                loads[half].wait()

            def body(at, half=half, weight=weight):
                sums = jnp.dot(
                    rows[k].reshape(2 * count, width), weight[:, at], preferred_element_type=f32
                )
                pair_out[k, half, :, at] = pick(sums, 1 - low).astype(bf16)
                kept_sums[slot, half, :, at] = pick(sums, low)

            over_tiles(units, body)
        send(2, k, pair_out.at[k], pair_in.at[k], core_peer)

    def second_sums(k):
        receive(2, k, pair_in.at[k], core_peer)
        at = pl.ds(pl.multiple_of((1 - high) * part, part), part)
        for half in range(2):
            across_out[k, half] = (
                kept_sums[k % 4, half, at, :] + pair_in[k, half, at, :].astype(f32)
            ).astype(bf16)
        send(3, k, across_out.at[k], across_in.at[k], across_peer)

    mine = low * count + high * part
    swapped = low * count + (1 - high) * part

    def act_rows(k, start):
        return act.at[k, pl.ds(pl.multiple_of(start, part), part), :]

    def activate(k):
        receive(3, k, across_in.at[k], across_peer)
        at = pl.ds(pl.multiple_of(high * part, part), part)
        gate, up = [
            kept_sums[k % 4, half, at, :]
            + pair_in[k, half, at, :].astype(f32)
            + across_in[k, half].astype(f32)
            for half in range(2)
        ]
        value = (gate / (1.0 + jnp.exp(-gate)) * up).astype(bf16)
        act[k, pl.ds(pl.multiple_of(mine, part), part), :] = value
        send(4, k, act_rows(k, mine), act_rows(k, mine), across_peer)
        send(5, k, act_rows(k, mine), act_rows(k, mine), core_peer)

    def down_terms(k):
        receive(4, k, act_rows(k, swapped), across_peer)
        send(6, k, act_rows(k, swapped), act_rows(k, swapped), core_peer)
        receive(5, k, act_rows(k, (1 - low) * count + high * part), core_peer)
        receive(6, k, act_rows(k, (1 - low) * count + (1 - high) * part), core_peer)
        if k == 0:
            loads[2].wait()

        def body(at):
            terms = jnp.dot(act[k], w_down[:, at], preferred_element_type=f32)
            term_out[k, :, at] = pick(terms, 1 - pair).astype(bf16)
            kept_down[k % 2, :, at] = pick(terms, pair)

        over_tiles(width, body)
        send(7, k, term_out.at[k], term_in.at[k], pair_peer)

    def pass_on(k):
        receive(7, k, term_in.at[k], pair_peer)
        value = kept_down[k % 2] + term_in[k].astype(f32)
        if k < pieces:
            total[piece(k)] = value
            return
        sum_out[k] = value.astype(bf16)
        send(8, k, sum_out.at[k], sum_in.at[k], column_peer(k // pieces))

    for step in range(chunks + 4):
        if step < chunks:
            first_sums(step)
            second_sums(step)
            if pieces <= step + 1 < chunks:
                forward(step + 1)
        for behind, stage in ((2, activate), (3, down_terms), (4, pass_on)):
            if 0 <= step - behind < chunks:
                stage(step - behind)
    for h in range(pieces):
        at = piece(h)
        down = total[at]
        for k in range(h + pieces, chunks, pieces):
            receive(8, k, sum_in.at[k], column_peer(k // pieces))
            down += sum_in[k].astype(f32)
        out_ref[at] = jnp.where(
            live_ref[at] > 0.0, residual_ref[at].astype(f32) + down, 0.0
        ).astype(bf16)
    for descriptor in started:
        descriptor.wait_send()


def feed_forward(normed_part, residual_part, live, w_gate, w_up, w_down):
    bf16, f32 = jnp.bfloat16, jnp.float32
    columns = lax.axis_size("req") // 2
    count, width = normed_part.shape
    units = w_gate.shape[1]
    total_rows = count
    pieces = 2 if columns <= 4 else 1
    chunks = columns * pieces
    count = count // pieces
    in_vmem = pl.BlockSpec(memory_space=pltpu.VMEM)
    anywhere = pl.BlockSpec(memory_space=pl.ANY)
    return pl.pallas_call(
        functools.partial(feed_forward_kernel, columns),
        name="feed_forward",
        out_shape=jax.ShapeDtypeStruct((total_rows, width), bf16),
        in_specs=[in_vmem] * 3 + [anywhere] * 3,
        out_specs=in_vmem,
        scratch_shapes=[
            pltpu.VMEM(w_gate.shape, bf16),
            pltpu.VMEM(w_up.shape, bf16),
            pltpu.VMEM(w_down.shape, bf16),
            pltpu.VMEM((chunks, 2, count, width), bf16),
            pltpu.VMEM((4, 2, count, units), f32),
            pltpu.VMEM((chunks, 2, count, units), bf16),
            pltpu.VMEM((chunks, 2, count, units), bf16),
            pltpu.VMEM((chunks, 2, count // 2, units), bf16),
            pltpu.VMEM((chunks, 2, count // 2, units), bf16),
            pltpu.VMEM((chunks, 2 * count, units), bf16),
            pltpu.VMEM((2, count, width), f32),
            pltpu.VMEM((chunks, count, width), bf16),
            pltpu.VMEM((chunks, count, width), bf16),
            pltpu.VMEM((chunks, count, width), bf16),
            pltpu.VMEM((chunks, count, width), bf16),
            pltpu.VMEM((total_rows, width), f32),
            pltpu.SemaphoreType.DMA((3,)),
            pltpu.SemaphoreType.DMA((9, chunks)),
            pltpu.SemaphoreType.DMA((9, chunks)),
        ],
        compiler_params=pltpu.CompilerParams(
            collective_id=0, has_side_effects=True, vmem_limit_bytes=60 * 1024 * 1024
        ),
    )(normed_part, residual_part, live, w_gate, w_up, w_down)


def shards(
    hidden_in,
    attn_gain,
    w_query,
    w_key,
    w_value,
    w_out,
    mlp_gain,
    w_gate,
    w_up,
    w_down,
    prefix_kv,
    suffix_lengths,
    prefix_owner,
):
    f32 = jnp.float32
    bf16 = jnp.bfloat16
    slots_here = hidden_in.shape[0]
    width = hidden_in.shape[1]
    head_dim = HEAD_DIM
    kv_heads = w_key.shape[1] // head_dim
    q_heads = w_query.shape[1] // head_dim
    group = q_heads // kv_heads
    block_len = prefix_kv.shape[0]
    width_part = w_gate.shape[0]
    mlp_at = lax.axis_index("mlp")
    low, high = mlp_at % 2, mlp_at // 2
    width_start = mlp_at * width_part
    request_of, live, positions = slot_layout(suffix_lengths[0], slots_here)
    hidden_f = hidden_in.astype(f32)
    normed = rms_norm(hidden_f, attn_gain).astype(bf16)
    query_rows = rope(
        jnp.dot(normed, w_query, preferred_element_type=f32).reshape(
            slots_here, q_heads, head_dim
        ),
        positions,
    ).astype(bf16)
    all_queries = [query_rows] + [from_xor(query_rows, "req", mask) for mask in range(1, GSPAN)]
    key_rows = rope(
        jnp.dot(normed, w_key, preferred_element_type=f32).reshape(slots_here, kv_heads, head_dim),
        positions,
    ).astype(bf16)
    value_rows = (
        jnp.dot(normed, w_value, preferred_element_type=f32)
        .astype(bf16)
        .reshape(slots_here, kv_heads, head_dim)
    )
    place = lax.axis_index("req") % GSPAN
    group_id = lax.axis_index("req") // GSPAN
    owners = lax.dynamic_index_in_dim(prefix_owner, group_id, 0, keepdims=False)
    quarter = jnp.sum(jnp.where(owners == place, jnp.arange(GSPAN, dtype=jnp.int32), 0))
    table = lax.dynamic_slice_in_dim(
        jnp.asarray(prefix_tables(head_dim)), quarter * block_len, block_len, 0
    )
    cosine, sine = table[:, None, : head_dim // 2], table[:, None, head_dim // 2 :]
    stored = prefix_kv[:, 0].reshape(block_len, kv_heads, head_dim).astype(f32)
    former, latter = stored[..., : head_dim // 2], stored[..., head_dim // 2 :]
    stored_keys = jnp.concatenate(
        [former * cosine - latter * sine, latter * cosine + former * sine], axis=-1
    ).astype(bf16)
    stored_values = prefix_kv[:, 1].reshape(block_len, kv_heads, head_dim)
    slot_ids = jnp.arange(slots_here, dtype=jnp.int32)
    allowed = (request_of[:, None] == request_of[None, :]) & (
        slot_ids[None, :] <= slot_ids[:, None]
    )
    outs, tops = [], []
    for mask in range(GSPAN):
        grouped = all_queries[mask].reshape(slots_here, kv_heads, group, head_dim)
        out, top = partial_attention(grouped, stored_keys, stored_values, None)
        if mask:
            out = from_xor(out.astype(bf16), "req", mask).astype(f32)
            top = from_xor(top, "req", mask)
        outs.append(out)
        tops.append(top)
    out, top = partial_attention(
        query_rows.reshape(slots_here, kv_heads, group, head_dim), key_rows, value_rows, allowed
    )
    outs.append(out)
    tops.append(top)
    highest = tops[0]
    for top in tops[1:]:
        highest = jnp.maximum(highest, top)
    merged, total = 0.0, 0.0
    for out, top in zip(outs, tops):
        share = jnp.exp(top - highest)
        merged += out * share[..., None]
        total += share
    attended = (
        jnp.transpose(merged / total[..., None], (2, 0, 1, 3))
        .reshape(slots_here, q_heads * head_dim)
        .astype(bf16)
    )

    def term_part(index):
        start = index * width_part
        return jnp.dot(
            attended,
            lax.dynamic_slice_in_dim(w_out, start, width_part, 1),
            preferred_element_type=f32,
        )

    away, home = (1 - high) * 2, high * 2
    away_in = from_xor(term_part(away + 1 - low).astype(bf16), "mlp", 1)
    home_in = from_xor(term_part(home + 1 - low).astype(bf16), "mlp", 1)
    away_out = (term_part(away + low) + away_in.astype(f32)).astype(bf16)
    across = from_xor(away_out, "mlp", 2)
    head_total = term_part(home + low) + home_in.astype(f32) + across.astype(f32)
    hidden_part = lax.dynamic_slice_in_dim(hidden_in, width_start, width_part, 1)
    residual_part = (hidden_part.astype(f32) + head_total).astype(bf16)
    residual_f = residual_part.astype(f32)
    squares = jnp.sum(residual_f * residual_f, axis=-1)
    squares += from_xor(squares, "mlp", 1)
    squares += from_xor(squares, "mlp", 2)
    gain_part = lax.dynamic_slice_in_dim(mlp_gain, width_start, width_part, 0)
    normed_part = (
        residual_f * lax.rsqrt(squares / width + eps)[:, None] * gain_part.astype(f32)
    ).astype(bf16)

    hidden_out = feed_forward(
        normed_part, residual_part, live.astype(f32)[:, None], w_gate, w_up, w_down
    )
    stacked_kv = jnp.stack(
        [
            key_rows.reshape(slots_here, kv_heads * head_dim),
            value_rows.reshape(slots_here, kv_heads * head_dim),
        ],
        axis=1,
    )
    suffix_kv = jnp.where(live[:, None, None], stacked_kv, jnp.zeros_like(stacked_kv))
    return (hidden_out, suffix_kv)


def solution(mesh):
    placed = (
        P("req", None),
        P(),
        P(None, "mlp"),
        P(None, "mlp"),
        P(None, "mlp"),
        P("mlp", None),
        P(),
        P("mlp", "req"),
        P("mlp", "req"),
        P("req", "mlp"),
        P("req", None, "mlp"),
        P("req", None),
        P(),
    )
    return jax.shard_map(
        shards,
        mesh=mesh,
        in_specs=placed,
        out_specs=(P("req", "mlp"), P("req", None, "mlp")),
        check_vma=False,
    )
```

```python
import functools
import math

import jax
import jax.numpy as jnp
import numpy as np
from jax import lax
from jax.experimental import pallas as pl
from jax.experimental.pallas import tpu as pltpu
from jax.sharding import PartitionSpec as P

HEAD_DIM = 128
PREFIX = 8192
GSPAN = 4


rope_base = 500000.0
eps = 1e-05


def from_xor(value, axis, mask):
    pairs = [(source, source ^ mask) for source in range(lax.axis_size(axis))]
    return lax.ppermute(value, axis, pairs)


def rope(values, positions):
    half = values.shape[-1] // 2
    freq = rope_base ** (-jnp.arange(half, dtype=jnp.float32) * 2.0 / values.shape[-1])
    angle = positions.astype(jnp.float32)[:, None] * freq[None, :]
    cosine = jnp.cos(angle)[:, None, :]
    sine = jnp.sin(angle)[:, None, :]
    former = values[..., :half]
    latter = values[..., half:]
    return jnp.concatenate(
        [former * cosine - latter * sine, latter * cosine + former * sine], axis=-1
    )


def prefix_tables(head_dim):
    half = head_dim // 2
    exponents = -np.arange(half, dtype=np.float32) * np.float32(2.0) / np.float32(head_dim)
    freq = np.power(np.float32(rope_base), exponents).astype(np.float32)
    angle = np.arange(PREFIX, dtype=np.float32)[:, None] * freq[None, :]
    return np.concatenate([np.cos(angle), np.sin(angle)], axis=1).astype(np.float32)


def rms_norm(values, gain):
    return (
        values
        * lax.rsqrt(jnp.mean(values * values, axis=-1, keepdims=True) + eps)
        * gain.astype(jnp.float32)
    )


def slot_layout(lengths, slot_count):
    ends = jnp.cumsum(lengths)
    starts = ends - lengths
    slot_ids = jnp.arange(slot_count, dtype=jnp.int32)
    request_of = jnp.sum((slot_ids[:, None] >= ends[None, :]).astype(jnp.int32), axis=1)
    picks = (request_of[:, None] == jnp.arange(lengths.shape[0], dtype=jnp.int32)[None, :]).astype(
        jnp.int32
    )
    start_of = jnp.sum(picks * starts[None, :], axis=1)
    positions = PREFIX + slot_ids - start_of
    return (request_of, request_of < lengths.shape[0], positions)


def partial_attention(grouped_queries, key_block, value_block, allowed):
    scores = jnp.einsum(
        "qkgd,nkd->kgqn", grouped_queries, key_block, preferred_element_type=jnp.float32
    ) / math.sqrt(grouped_queries.shape[-1])
    if allowed is not None:
        scores = jnp.where(allowed[None, None], scores, -jnp.inf)
    peak = jnp.max(scores, axis=-1)
    weights = jnp.exp(scores - peak[..., None])
    weight_sum = jnp.sum(weights, axis=-1)
    summed = jnp.einsum(
        "kgqn,nkd->kgqd",
        weights.astype(jnp.bfloat16),
        value_block,
        preferred_element_type=jnp.float32,
    )
    return (summed / weight_sum[..., None], peak + jnp.log(weight_sum))


def tile_of(size):
    return 256 if size % 256 == 0 else size


def over_tiles(size, body):
    tile = tile_of(size)
    if size == tile:
        body(pl.ds(0, tile))
        return

    @pl.loop(0, size // tile)
    def _(index):
        body(pl.ds(pl.multiple_of(index * tile, tile), tile))


def feed_forward_kernel(
    columns,
    normed_ref,
    residual_ref,
    live_ref,
    gate_hbm,
    up_hbm,
    down_hbm,
    out_ref,
    w_gate,
    w_up,
    w_down,
    rows,
    kept_sums,
    pair_out,
    pair_in,
    across_out,
    across_in,
    act,
    kept_down,
    term_out,
    term_in,
    sum_out,
    sum_in,
    total,
    weight_sems,
    send_sems,
    recv_sems,
):
    f32, bf16 = jnp.float32, jnp.bfloat16
    req, mlp = lax.axis_index("req"), lax.axis_index("mlp")
    column, pair = lax.div(req, 2), lax.rem(req, 2)
    high, low = lax.div(mlp, 2), lax.rem(mlp, 2)
    pieces = rows.shape[0] // columns
    chunks = columns * pieces
    count = normed_ref.shape[0] // pieces
    part = count // 2
    width = normed_ref.shape[1]
    units = w_gate.shape[1]
    pair_peer = (column * 2 + 1 - pair, mlp)
    core_peer = (req, high * 2 + 1 - low)
    across_peer = (req, (1 - high) * 2 + low)

    def column_peer(mask):
        other = column
        for bit in range(columns.bit_length() - 1):
            if mask >> bit & 1:
                other += (1 - 2 * lax.rem(lax.div(column, 1 << bit), 2)) * (1 << bit)
        return (other * 2 + pair, mlp)

    def piece(k):
        return pl.ds(k % pieces * count, count)

    def copy(kind, k, src, dst, peer):
        return pltpu.make_async_remote_copy(
            src_ref=src,
            dst_ref=dst,
            send_sem=send_sems.at[kind, k],
            recv_sem=recv_sems.at[kind, k],
            device_id=peer,
            device_id_type=pl.DeviceIdType.MESH,
        )

    started = []

    def send(kind, k, src, dst, peer):
        descriptor = copy(kind, k, src, dst, peer)
        descriptor.start()
        started.append(descriptor)

    def receive(kind, k, dst, peer):
        copy(kind, k, dst, dst, peer).wait_recv()

    loads = [
        pltpu.make_async_copy(source, target, weight_sems.at[index])
        for index, (source, target) in enumerate(
            [(gate_hbm, w_gate), (up_hbm, w_up), (down_hbm, w_down)]
        )
    ]
    for load in loads:
        load.start()

    barrier = pltpu.get_barrier_semaphore()
    peers = [pair_peer, core_peer, across_peer] + [column_peer(k) for k in range(1, columns)]
    for peer in peers:
        pl.semaphore_signal(barrier, inc=1, device_id=peer, device_id_type=pl.DeviceIdType.MESH)
    pl.semaphore_wait(barrier, len(peers))

    for k in range(chunks):
        if k < pieces:
            send(1, k, normed_ref.at[piece(k)], rows.at[k, pair], pair_peer)
            rows[k, pair] = normed_ref[piece(k)]
        else:
            send(0, k, normed_ref.at[piece(k)], rows.at[k, pair], column_peer(k // pieces))

    def forward(k):
        receive(0, k, rows.at[k, pair], column_peer(k // pieces))
        send(1, k, rows.at[k, pair], rows.at[k, pair], pair_peer)

    def pick(value, which):
        return jnp.where(which == 0, value[:count], value[count:])

    def first_sums(k):
        receive(1, k, rows.at[k, 1 - pair], pair_peer)
        slot = k % 4
        for half, weight in enumerate((w_gate, w_up)):
            if k == 0:
                loads[half].wait()

            def body(at, half=half, weight=weight):
                sums = jnp.dot(
                    rows[k].reshape(2 * count, width), weight[:, at], preferred_element_type=f32
                )
                pair_out[k, half, :, at] = pick(sums, 1 - low).astype(bf16)
                kept_sums[slot, half, :, at] = pick(sums, low)

            over_tiles(units, body)
        send(2, k, pair_out.at[k], pair_in.at[k], core_peer)

    def second_sums(k):
        receive(2, k, pair_in.at[k], core_peer)
        at = pl.ds(pl.multiple_of((1 - high) * part, part), part)
        for half in range(2):
            across_out[k, half] = (
                kept_sums[k % 4, half, at, :] + pair_in[k, half, at, :].astype(f32)
            ).astype(bf16)
        send(3, k, across_out.at[k], across_in.at[k], across_peer)

    mine = low * count + high * part
    swapped = low * count + (1 - high) * part

    def act_rows(k, start):
        return act.at[k, pl.ds(pl.multiple_of(start, part), part), :]

    def activate(k):
        receive(3, k, across_in.at[k], across_peer)
        at = pl.ds(pl.multiple_of(high * part, part), part)
        gate, up = [
            kept_sums[k % 4, half, at, :]
            + pair_in[k, half, at, :].astype(f32)
            + across_in[k, half].astype(f32)
            for half in range(2)
        ]
        value = (gate / (1.0 + jnp.exp(-gate)) * up).astype(bf16)
        act[k, pl.ds(pl.multiple_of(mine, part), part), :] = value
        send(4, k, act_rows(k, mine), act_rows(k, mine), across_peer)
        send(5, k, act_rows(k, mine), act_rows(k, mine), core_peer)

    def down_terms(k):
        receive(4, k, act_rows(k, swapped), across_peer)
        send(6, k, act_rows(k, swapped), act_rows(k, swapped), core_peer)
        receive(5, k, act_rows(k, (1 - low) * count + high * part), core_peer)
        receive(6, k, act_rows(k, (1 - low) * count + (1 - high) * part), core_peer)
        if k == 0:
            loads[2].wait()

        def body(at):
            terms = jnp.dot(act[k], w_down[:, at], preferred_element_type=f32)
            term_out[k, :, at] = pick(terms, 1 - pair).astype(bf16)
            kept_down[k % 2, :, at] = pick(terms, pair)

        over_tiles(width, body)
        send(7, k, term_out.at[k], term_in.at[k], pair_peer)

    def pass_on(k):
        receive(7, k, term_in.at[k], pair_peer)
        value = kept_down[k % 2] + term_in[k].astype(f32)
        if k < pieces:
            total[piece(k)] = value
            return
        sum_out[k] = value.astype(bf16)
        send(8, k, sum_out.at[k], sum_in.at[k], column_peer(k // pieces))

    for step in range(chunks + 5):
        if step < chunks:
            first_sums(step)
        if pieces <= step - 1 < chunks or 0 <= step - 1 < pieces - 1:
            second_sums(step - 1)
        if step == pieces - 1:
            second_sums(step)
        if pieces <= step + 1 < chunks:
            forward(step + 1)
        for behind, stage in ((3, activate), (4, down_terms), (5, pass_on)):
            if 0 <= step - behind < chunks:
                stage(step - behind)
    for h in range(pieces):
        at = piece(h)
        down = total[at]
        for k in range(h + pieces, chunks, pieces):
            receive(8, k, sum_in.at[k], column_peer(k // pieces))
            down += sum_in[k].astype(f32)
        out_ref[at] = jnp.where(
            live_ref[at] > 0.0, residual_ref[at].astype(f32) + down, 0.0
        ).astype(bf16)
    for descriptor in started:
        descriptor.wait_send()


def feed_forward(normed_part, residual_part, live, w_gate, w_up, w_down):
    bf16, f32 = jnp.bfloat16, jnp.float32
    columns = lax.axis_size("req") // 2
    count, width = normed_part.shape
    units = w_gate.shape[1]
    total_rows = count
    pieces = 2 if columns <= 4 else 1
    chunks = columns * pieces
    count = count // pieces
    in_vmem = pl.BlockSpec(memory_space=pltpu.VMEM)
    anywhere = pl.BlockSpec(memory_space=pl.ANY)
    return pl.pallas_call(
        functools.partial(feed_forward_kernel, columns),
        name="feed_forward",
        out_shape=jax.ShapeDtypeStruct((total_rows, width), bf16),
        in_specs=[in_vmem] * 3 + [anywhere] * 3,
        out_specs=in_vmem,
        scratch_shapes=[
            pltpu.VMEM(w_gate.shape, bf16),
            pltpu.VMEM(w_up.shape, bf16),
            pltpu.VMEM(w_down.shape, bf16),
            pltpu.VMEM((chunks, 2, count, width), bf16),
            pltpu.VMEM((4, 2, count, units), f32),
            pltpu.VMEM((chunks, 2, count, units), bf16),
            pltpu.VMEM((chunks, 2, count, units), bf16),
            pltpu.VMEM((chunks, 2, count // 2, units), bf16),
            pltpu.VMEM((chunks, 2, count // 2, units), bf16),
            pltpu.VMEM((chunks, 2 * count, units), bf16),
            pltpu.VMEM((2, count, width), f32),
            pltpu.VMEM((chunks, count, width), bf16),
            pltpu.VMEM((chunks, count, width), bf16),
            pltpu.VMEM((chunks, count, width), bf16),
            pltpu.VMEM((chunks, count, width), bf16),
            pltpu.VMEM((total_rows, width), f32),
            pltpu.SemaphoreType.DMA((3,)),
            pltpu.SemaphoreType.DMA((9, chunks)),
            pltpu.SemaphoreType.DMA((9, chunks)),
        ],
        compiler_params=pltpu.CompilerParams(
            collective_id=0, has_side_effects=True, vmem_limit_bytes=60 * 1024 * 1024
        ),
    )(normed_part, residual_part, live, w_gate, w_up, w_down)


def shards(
    hidden_in,
    attn_gain,
    w_query,
    w_key,
    w_value,
    w_out,
    mlp_gain,
    w_gate,
    w_up,
    w_down,
    prefix_kv,
    suffix_lengths,
    prefix_owner,
):
    f32 = jnp.float32
    bf16 = jnp.bfloat16
    slots_here = hidden_in.shape[0]
    width = hidden_in.shape[1]
    head_dim = HEAD_DIM
    kv_heads = w_key.shape[1] // head_dim
    q_heads = w_query.shape[1] // head_dim
    group = q_heads // kv_heads
    block_len = prefix_kv.shape[0]
    width_part = w_gate.shape[0]
    mlp_at = lax.axis_index("mlp")
    low, high = mlp_at % 2, mlp_at // 2
    width_start = mlp_at * width_part
    request_of, live, positions = slot_layout(suffix_lengths[0], slots_here)
    hidden_f = hidden_in.astype(f32)
    normed = rms_norm(hidden_f, attn_gain).astype(bf16)
    query_rows = rope(
        jnp.dot(normed, w_query, preferred_element_type=f32).reshape(
            slots_here, q_heads, head_dim
        ),
        positions,
    ).astype(bf16)
    all_queries = [query_rows] + [from_xor(query_rows, "req", mask) for mask in range(1, GSPAN)]
    key_rows = rope(
        jnp.dot(normed, w_key, preferred_element_type=f32).reshape(slots_here, kv_heads, head_dim),
        positions,
    ).astype(bf16)
    value_rows = (
        jnp.dot(normed, w_value, preferred_element_type=f32)
        .astype(bf16)
        .reshape(slots_here, kv_heads, head_dim)
    )
    place = lax.axis_index("req") % GSPAN
    group_id = lax.axis_index("req") // GSPAN
    owners = lax.dynamic_index_in_dim(prefix_owner, group_id, 0, keepdims=False)
    quarter = jnp.sum(jnp.where(owners == place, jnp.arange(GSPAN, dtype=jnp.int32), 0))
    table = lax.dynamic_slice_in_dim(
        jnp.asarray(prefix_tables(head_dim)), quarter * block_len, block_len, 0
    )
    cosine, sine = table[:, None, : head_dim // 2], table[:, None, head_dim // 2 :]
    stored = prefix_kv[:, 0].reshape(block_len, kv_heads, head_dim).astype(f32)
    former, latter = stored[..., : head_dim // 2], stored[..., head_dim // 2 :]
    stored_keys = jnp.concatenate(
        [former * cosine - latter * sine, latter * cosine + former * sine], axis=-1
    ).astype(bf16)
    stored_values = prefix_kv[:, 1].reshape(block_len, kv_heads, head_dim)
    slot_ids = jnp.arange(slots_here, dtype=jnp.int32)
    allowed = (request_of[:, None] == request_of[None, :]) & (
        slot_ids[None, :] <= slot_ids[:, None]
    )
    outs, tops = [], []
    for mask in range(GSPAN):
        grouped = all_queries[mask].reshape(slots_here, kv_heads, group, head_dim)
        out, top = partial_attention(grouped, stored_keys, stored_values, None)
        if mask:
            out = from_xor(out.astype(bf16), "req", mask).astype(f32)
            top = from_xor(top, "req", mask)
        outs.append(out)
        tops.append(top)
    out, top = partial_attention(
        query_rows.reshape(slots_here, kv_heads, group, head_dim), key_rows, value_rows, allowed
    )
    outs.append(out)
    tops.append(top)
    highest = tops[0]
    for top in tops[1:]:
        highest = jnp.maximum(highest, top)
    merged, total = 0.0, 0.0
    for out, top in zip(outs, tops):
        share = jnp.exp(top - highest)
        merged += out * share[..., None]
        total += share
    attended = (
        jnp.transpose(merged / total[..., None], (2, 0, 1, 3))
        .reshape(slots_here, q_heads * head_dim)
        .astype(bf16)
    )

    head_terms = jnp.dot(attended, w_out, preferred_element_type=f32)

    def term_part(index):
        return lax.dynamic_slice_in_dim(head_terms, index * width_part, width_part, 1)

    away, home = (1 - high) * 2, high * 2
    away_in = from_xor(term_part(away + 1 - low).astype(bf16), "mlp", 1)
    home_in = from_xor(term_part(home + 1 - low).astype(bf16), "mlp", 1)
    away_out = (term_part(away + low) + away_in.astype(f32)).astype(bf16)
    across = from_xor(away_out, "mlp", 2)
    head_total = term_part(home + low) + home_in.astype(f32) + across.astype(f32)
    hidden_part = lax.dynamic_slice_in_dim(hidden_in, width_start, width_part, 1)
    residual_part = (hidden_part.astype(f32) + head_total).astype(bf16)
    residual_f = residual_part.astype(f32)
    squares = jnp.sum(residual_f * residual_f, axis=-1)
    squares += from_xor(squares, "mlp", 1)
    squares += from_xor(squares, "mlp", 2)
    gain_part = lax.dynamic_slice_in_dim(mlp_gain, width_start, width_part, 0)
    normed_part = (
        residual_f * lax.rsqrt(squares / width + eps)[:, None] * gain_part.astype(f32)
    ).astype(bf16)

    hidden_out = feed_forward(
        normed_part, residual_part, live.astype(f32)[:, None], w_gate, w_up, w_down
    )
    stacked_kv = jnp.stack(
        [
            key_rows.reshape(slots_here, kv_heads * head_dim),
            value_rows.reshape(slots_here, kv_heads * head_dim),
        ],
        axis=1,
    )
    suffix_kv = jnp.where(live[:, None, None], stacked_kv, jnp.zeros_like(stacked_kv))
    return (hidden_out, suffix_kv)


def solution(mesh):
    placed = (
        P("req", None),
        P(),
        P(None, "mlp"),
        P(None, "mlp"),
        P(None, "mlp"),
        P("mlp", None),
        P(),
        P("mlp", "req"),
        P("mlp", "req"),
        P("req", "mlp"),
        P("req", None, "mlp"),
        P("req", None),
        P(),
    )
    return jax.shard_map(
        shards,
        mesh=mesh,
        in_specs=placed,
        out_specs=(P("req", "mlp"), P("req", None, "mlp")),
        check_vma=False,
    )
```
